256 devices in a mesh: rows: 8 (over x_lo, y), pairs: 32 (over z, x_hi, core).
Axes of the slice: x: 4 (x_hi: 2, x_lo: 2; x = x_hi * 2 + x_lo), y: 4, z: 8, core: 2. Of those that a mesh axis runs over, the one named last changes fastest.
Arguments:
- matrix: float32 [32768, 8192], P('rows', 'pairs'), may hold values from -6 to 6
- vectors: float32 [8192, 8192], P('rows', 'pairs'), may hold values from -6 to 6
Outputs:
- matrix_out: float32 [32768, 8192], P('rows', 'pairs')
- vectors_out: float32 [8192, 8192], P('rows', 'pairs')
The draws below stay inside these ranges and needn't reach their ends.
All inputs are finite; a program needn't handle non-finite values.
Results may differ from the reference program's by a relative error of at most 0.0029.
Values sent between devices are 32-bit elements; how exact they have to be, the bound alone decides.
A program may use at most 64 MiB of HBM per device.

```python
import jax
import jax.numpy as jnp
import numpy as np
from jax import lax

B = 128
STEPS = 16
ROUNDS = 2
ROWS_ALL = 32768
COLS = 8192
N_PAIRS = 32


def level_of(stream_key, dims, pieces, smallest, high):
    def one(dim, parts):
        heights = jax.random.uniform(jax.random.fold_in(jax.random.fold_in(stream_key, 6), dim), (parts,), jnp.float32, smallest / len(pieces), high / len(pieces))
        return jnp.repeat(jnp.exp(heights), dims[dim] // parts).reshape((-1,) + (1,) * (len(dims) - dim - 1))

    gain = one(*pieces[0])
    for cut in pieces[1:]:
        gain = gain * one(*cut)
    return gain


def gaussian(stream_key, shape, spread, most, pieces=(), kind=jnp.bfloat16):
    values = spread * jax.random.normal(stream_key, shape, jnp.float32)
    if pieces:
        values = values * level_of(stream_key, shape, pieces, -0.22, 0.18)
    return jnp.clip(values, -most, most).astype(kind)


def setup_inputs(seed: int = 0) -> dict:
    splits = jax.random.split(jax.random.key(seed), 3)
    return {
        "matrix": gaussian(splits[0], (ROWS_ALL, COLS), 1.0, 6.0, ((0, 8), (1, 32)), jnp.float32),
        "vectors": gaussian(splits[1], (COLS, COLS), 1.0, 6.0, ((0, 8), (1, 32)), jnp.float32),
    }


def rotate_cols(block, cosine, sine, half):
    left = block[:, :half]
    right = block[:, half:]
    return jnp.concatenate([left * cosine + right * sine, right * cosine - left * sine], axis=1)


def rotate_rows(block, cosine, sine, half):
    upper = block[:half, :]
    lower = block[half:, :]
    cos_col = cosine[:, None]
    sin_col = sine[:, None]
    return jnp.concatenate([upper * cos_col + lower * sin_col, lower * cos_col - upper * sin_col], axis=0)


def permute_axis(block, axis, half):
    width = 2 * half
    first = lax.slice_in_dim(block, 0, 1, axis=axis)
    second = lax.slice_in_dim(block, half, half + 1, axis=axis)
    upper = lax.slice_in_dim(block, 1, half - 1, axis=axis)
    lower = lax.slice_in_dim(block, half + 1, width, axis=axis)
    final = lax.slice_in_dim(block, half - 1, half, axis=axis)
    return jnp.concatenate([first, second, upper, lower, final], axis=axis)


def source_table(width):
    half = width // 2
    source = np.zeros(width, dtype=np.int64)
    source[0] = 0
    source[1] = half
    source[2:half] = np.arange(1, half - 1)
    source[half:width - 1] = np.arange(half + 1, width)
    source[width - 1] = half - 1
    return source


def jacobi(gram, steps):
    width = gram.shape[0]
    half = width // 2
    source = source_table(width)
    order = np.arange(width)
    for turn in range(steps):
        order = order[source]
    inverse = np.argsort(order).astype(np.int32)
    basis = jnp.eye(width, dtype=gram.dtype)

    def one_step(index, state):
        current, accum = state
        diag = jnp.diagonal(current)
        cross = jnp.diagonal(current[:half, half:])
        angle = 0.5 * jnp.arctan2(2.0 * cross, diag[:half] - diag[half:])
        cosine = jnp.cos(angle)
        sine = jnp.sin(angle)
        current = rotate_cols(current, cosine, sine, half)
        current = rotate_rows(current, cosine, sine, half)
        accum = rotate_cols(accum, cosine, sine, half)
        current = permute_axis(permute_axis(current, 0, half), 1, half)
        accum = permute_axis(accum, 1, half)
        return current, accum

    current, accum = lax.fori_loop(0, steps, one_step, (gram, basis))
    current = jnp.take(jnp.take(current, inverse, axis=0), inverse, axis=1)
    accum = jnp.take(accum, inverse, axis=1)
    return current, accum


def advance(stack, half):
    tops = stack[:, :, :half]
    bottoms = stack[:, :, half:]
    new_tops = jnp.concatenate([tops[:1], bottoms[:1], tops[1:-1]], axis=0)
    new_bottoms = jnp.concatenate([bottoms[1:], tops[-1:]], axis=0)
    return jnp.concatenate([new_tops, new_bottoms], axis=2)


def reference(matrix, vectors):
    width = 2 * B
    blocks = matrix.reshape(ROWS_ALL, N_PAIRS, width).transpose(1, 0, 2)
    vblocks = vectors.reshape(COLS, N_PAIRS, width).transpose(1, 0, 2)

    def solve_pair(item):
        panel, vpanel = item
        gram = lax.dot_general(panel, panel, (((0,), (0,)), ((), ())), precision=lax.Precision.HIGHEST, preferred_element_type=jnp.float32)
        rotated, basis = jacobi(gram, STEPS)
        new_panel = jnp.dot(panel, basis, precision=lax.Precision.HIGHEST, preferred_element_type=jnp.float32)
        new_vpanel = jnp.dot(vpanel, basis, precision=lax.Precision.HIGHEST, preferred_element_type=jnp.float32)
        return new_panel, new_vpanel

    for turn in range(ROUNDS):
        blocks, vblocks = lax.map(solve_pair, (blocks, vblocks))
        blocks = advance(blocks, B)
        vblocks = advance(vblocks, B)
    matrix_out = blocks.transpose(1, 0, 2).reshape(ROWS_ALL, COLS)
    vectors_out = vblocks.transpose(1, 0, 2).reshape(COLS, COLS)
    return matrix_out, vectors_out
```

```python
import functools

import jax
import jax.numpy as jnp
from jax import lax
from jax.experimental import pallas as pl
from jax.experimental.pallas import tpu as pltpu
from jax.sharding import PartitionSpec as P

STEPS = 16
H = 128
W = 2 * H
CHUNK = 512
MESH = pl.DeviceIdType.MESH
F32 = jnp.float32
BF16 = jnp.bfloat16


def iota(shape, axis):
    return lax.broadcasted_iota(jnp.int32, shape, axis)


def split(v):
    hi = v.astype(BF16)
    return hi, (v - hi.astype(F32)).astype(BF16)


def split3(v):
    hi = v.astype(BF16)
    rest = v - hi.astype(F32)
    mid = rest.astype(BF16)
    return hi, mid, (rest - mid.astype(F32)).astype(BF16)


def dot(a, b):
    return jnp.dot(a, b, preferred_element_type=F32)


def dot_t(a, b):
    return lax.dot_general(a, b, (((0,), (0,)), ((), ())), preferred_element_type=F32)


def diag_row(block):
    lane = iota((8, H), 1)
    sub = iota((8, H), 0)
    parts = []
    for g in range(4):
        acc = block[32 * g : 32 * g + 8]
        for i in range(4 * g + 1, 4 * g + 4):
            acc = jnp.where(lane // 8 == i, block[8 * i : 8 * i + 8], acc)
        parts.append(acc)
    low = jnp.where(lane < 32, parts[0], parts[1])
    high = jnp.where(lane < 96, parts[2], parts[3])
    both = jnp.where(lane < 64, low, high)
    return jnp.sum(jnp.where(lane % 8 == sub, both, 0.0), axis=0, keepdims=True)


def angles(x, y):
    m = jnp.maximum(jnp.abs(x), jnp.abs(y))
    g = pl.reciprocal(m, approx=True)
    xs = x * g
    ys = y * g
    s = xs * xs + ys * ys
    r = s * lax.rsqrt(s)
    h = r + jnp.abs(xs)
    w = lax.rsqrt(2.0 * r * h)
    big = h * w
    small = jnp.abs(ys) * w
    flat = x >= 0.0
    none = m == 0.0
    cs = jnp.where(none, 1.0, jnp.where(flat, big, small))
    sn = jnp.where(none, 0.0, jnp.where(flat, small, big))
    return cs, jnp.where(y < 0.0, -sn, sn)


def lane_move(left, right):
    lane0 = iota(left.shape, 1) == 0
    rolled = pltpu.roll(jnp.where(lane0, right, left), 1, 1)
    new_left = jnp.where(lane0, left, rolled)
    new_right = pltpu.roll(jnp.where(lane0, rolled, right), H - 1, 1)
    return new_left, new_right


def as_columns(cs, sn):
    t = jnp.transpose(jnp.where(iota((H, H), 0) < H // 2, cs, sn))
    o = pltpu.roll(t, H // 2, 1)
    near = iota((H, H), 1) < H // 2
    return jnp.where(near, t, o), jnp.where(near, o, t)


def store_rows(ref, up, lo):
    ref[H - 1 : W - 1, :] = lo
    ref[1:H, :] = up[0 : H - 1]
    ref[0:1, :] = up[0:1]
    ref[1:2, :] = lo[0:1]
    ref[W - 1 : W, :] = up[H - 1 : H]


def jacobi_start(state, a, c, c_t, b):
    gl, gr, ql, qr = state
    gl[0:H, :] = a
    gl[H:W, :] = c_t
    gr[0:H, :] = c
    gr[H:W, :] = b
    ql[...] = (iota((W, H), 0) == iota((W, H), 1)).astype(F32)
    qr[...] = (iota((W, H), 0) == iota((W, H), 1) + H).astype(F32)


def jacobi_step(state):
    gl, gr, ql, qr = state
    a, d, c, b = gl[0:H], gl[H:W], gr[0:H], gr[H:W]
    cs, sn = angles(diag_row(a) - diag_row(b), 2.0 * diag_row(c))
    cc, sc = as_columns(cs, sn)
    a, c = lane_move(a * cs + c * sn, c * cs - a * sn)
    d, b = lane_move(d * cs + b * sn, b * cs - d * sn)
    store_rows(gl, a * cc + d * sc, d * cc - a * sc)
    store_rows(gr, c * cc + b * sc, b * cc - c * sc)
    left, right = ql[...], qr[...]
    left, right = lane_move(left * cs + right * sn, right * cs - left * sn)
    ql[...] = left
    qr[...] = right


def home():
    j = iota((W, W), 1)
    at = jnp.where(j < H - STEPS, j + STEPS, 3 * H - STEPS - 1 - j)
    at = jnp.where(j >= H, H + STEPS - j, at)
    at = jnp.where(j >= H + STEPS, j - STEPS, at)
    at = jnp.where(j == 0, 0, at)
    return (iota((W, W), 0) == at).astype(F32).astype(BF16)


def basis_split(state, sel):
    ql, qr = state[2], state[3]
    lh, ll = split(ql[...])
    rh, rl = split(qr[...])
    high = dot(lh, sel[0:H]) + dot(rh, sel[H:W])
    low = dot(ll, sel[0:H]) + dot(rl, sel[H:W])
    return high.astype(BF16), low.astype(BF16)


def gram_blocks(state, sel):
    gl, gr = state[0], state[1]
    moved = sum(dot(l, sel[0:H]) + dot(r, sel[H:W]) for l, r in zip(split3(gl[...]), split3(gr[...])))
    parts = split3(moved)
    top = sum(dot_t(sel[:, 0:H], p[:, 0:H]) for p in parts)
    bottom = sum(dot_t(sel[:, H:W], p[:, H:W]) for p in parts)
    return top, bottom


def kernel(
    n_rows, n_pairs, m_rows, v_rows,
    matrix, vectors, matrix_out, vectors_out,
    panel, mine, inbox, acc, gs, rs1, ag1, diag, rs2src, rs2, ag2,
    a_gl, a_gr, a_ql, a_qr, b_gl, b_gr, b_ql, b_qr,
    load_sem, out_sem, send_sem, recv_sem, rs1_send, rs1_recv, ag1_send, ag1_recv,
    dg_send, dg_recv, rs2_send, rs2_recv, ag2_send, ag2_recv,
):
    me = lax.axis_index("rows")
    k = lax.axis_index("pairs")
    first, second = k == 0, k == 1
    last, before_last = k == n_pairs - 1, k == n_pairs - 2
    m_chunks, v_chunks = m_rows // CHUNK, v_rows // CHUNK
    chunks = m_chunks + v_chunks
    piece = H // n_rows
    mine_rows = pl.ds(pl.multiple_of(me * piece, piece), piece)

    u_to = jnp.where(last, k - 1, jnp.where(before_last, k + 1, k + 2))
    u_slot = jnp.where(k >= n_pairs - 2, 1, 0)
    v_to = jnp.where(first, 1, jnp.where(second, 0, k - 2))
    v_slot = jnp.where(k <= 1, 0, 1)
    l_from, r_from = v_to, u_to

    def load(c):
        rows = pl.ds(pl.multiple_of(c * CHUNK, CHUNK), CHUNK)
        return pltpu.make_async_copy(matrix.at[rows], panel.at[rows], load_sem.at[c])

    def load_v(c):
        rows = pl.ds(pl.multiple_of(c * CHUNK, CHUNK), CHUNK)
        at = pl.ds(pl.multiple_of(m_rows + c * CHUNK, CHUNK), CHUNK)
        return pltpu.make_async_copy(vectors.at[rows], panel.at[at], load_sem.at[m_chunks + c])

    def each(n, body):
        lax.fori_loop(0, n, lambda i, carry: (body(i), carry)[1], 0)

    each(m_chunks, lambda c: load(c).start())
    each(v_chunks, lambda c: load_v(c).start())

    barrier = pltpu.get_barrier_semaphore()
    for d in range(1, n_rows):
        pl.semaphore_signal(barrier, inc=1, device_id=(lax.rem(me + d, n_rows), k), device_id_type=MESH)
    pl.semaphore_signal(barrier, inc=1, device_id=(me, l_from), device_id_type=MESH)
    pl.semaphore_signal(barrier, inc=1, device_id=(me, r_from), device_id_type=MESH)

    acc[...] = jnp.zeros_like(acc)

    def gram_chunk(c):
        load(c).wait()
        hi, lo = split(panel[pl.ds(pl.multiple_of(c * CHUNK, CHUNK), CHUNK), :])
        acc[0] += dot_t(hi, hi)
        acc[1] += dot_t(hi, lo)

    each(m_chunks, gram_chunk)
    hl = acc[1]
    full = acc[0] + (hl + jnp.transpose(hl))
    gs[:, 0:H] = full[0:H, 0:H]
    gs[:, H:W] = full[0:H, H:W]
    gs[:, W:] = full[H:W, H:W]

    pl.semaphore_wait(barrier, n_rows + 1)

    def peer(d):
        return lax.rem(me + d, n_rows)

    def scatter(src, dst, send, recv):
        copies = []
        for d in range(1, n_rows):
            rows = pl.ds(pl.multiple_of(peer(d) * piece, piece), piece)
            copies.append(
                pltpu.make_async_remote_copy(
                    src_ref=src.at[rows], dst_ref=dst.at[d], send_sem=send.at[d], recv_sem=recv.at[d],
                    device_id=(peer(d), k), device_id_type=MESH,
                )
            )
        for copy in copies:
            copy.start()
        for copy in copies:
            copy.wait()
        total = src[mine_rows, :]
        for d in range(1, n_rows):
            total = total + dst[d]
        return total

    def gather(buf, send, recv):
        copies = []
        for d in range(1, n_rows):
            copies.append(
                pltpu.make_async_remote_copy(
                    src_ref=buf.at[mine_rows], dst_ref=buf.at[mine_rows], send_sem=send.at[d], recv_sem=recv.at[d],
                    device_id=(peer(d), k), device_id_type=MESH,
                )
            )
        for copy in copies:
            copy.start()
        for copy in copies:
            copy.wait()

    ag1[mine_rows, :] = scatter(gs, rs1, rs1_send, rs1_recv)
    gather(ag1, ag1_send, ag1_recv)

    state_a = (a_gl, a_gr, a_ql, a_qr)
    state_b = (b_gl, b_gr, b_ql, b_qr)
    c1 = ag1[:, H:W]
    jacobi_start(state_a, ag1[:, 0:H], c1, jnp.transpose(c1), ag1[:, W:])
    each(STEPS, lambda t: jacobi_step(state_a))
    sel = home()
    q_hi, q_lo = basis_split(state_a, sel)

    def swapped(q):
        q = q.astype(F32)
        left = jnp.where(first, q[:, H:W], q[:, 0:H])
        right = jnp.where(first, q[:, 0:H], q[:, H:W])
        return left.astype(BF16), right.astype(BF16)

    qu_hi, qv_hi = swapped(q_hi)
    qu_lo, qv_lo = swapped(q_lo)
    q_hi = jnp.concatenate([qu_hi, qv_hi], axis=1)
    q_lo = jnp.concatenate([qu_lo, qv_lo], axis=1)

    def rows_of(c):
        return pl.ds(pl.multiple_of(c * CHUNK, CHUNK), CHUNK)

    def send(side, c):
        to, slot = ((u_to, u_slot), (v_to, v_slot))[side]
        return pltpu.make_async_remote_copy(
            src_ref=mine.at[side, rows_of(c)], dst_ref=inbox.at[slot, rows_of(c)],
            send_sem=send_sem.at[side, c], recv_sem=recv_sem.at[slot, c],
            device_id=(me, to), device_id_type=MESH,
        )

    def receive(slot, c):
        return pltpu.make_async_remote_copy(
            src_ref=mine.at[slot, rows_of(c)], dst_ref=inbox.at[slot, rows_of(c)],
            send_sem=send_sem.at[slot, c], recv_sem=recv_sem.at[slot, c],
            device_id=(me, u_to), device_id_type=MESH,
        )

    each(v_chunks, lambda c: load_v(c).wait())

    def rotate_chunk(c):
        hi, lo = split(panel[rows_of(c), :])
        new = dot(hi, q_hi) + (dot(hi, q_lo) + dot(lo, q_hi))
        mine[0, rows_of(c), :] = new[:, 0:H]
        mine[1, rows_of(c), :] = new[:, H:W]
        send(0, c).start()
        send(1, c).start()

    each(m_chunks, rotate_chunk)

    top, bottom = gram_blocks(state_a, sel)
    diag[0] = jnp.where(first, bottom, top)
    diag[1] = jnp.where(first, top, bottom)

    def send_diag(side):
        to, slot = ((u_to, u_slot), (v_to, v_slot))[side]
        return pltpu.make_async_remote_copy(
            src_ref=diag.at[side, mine_rows], dst_ref=ag2.at[2 + slot, mine_rows],
            send_sem=dg_send.at[side], recv_sem=dg_recv.at[slot],
            device_id=(me, to), device_id_type=MESH,
        )

    def receive_diag(slot):
        return pltpu.make_async_remote_copy(
            src_ref=diag.at[slot, mine_rows], dst_ref=ag2.at[2 + slot, mine_rows],
            send_sem=dg_send.at[slot], recv_sem=dg_recv.at[slot],
            device_id=(me, u_to), device_id_type=MESH,
        )

    send_diag(0).start()
    send_diag(1).start()
    lax.fori_loop(m_chunks, chunks, lambda c, carry: (rotate_chunk(c), carry)[1], 0)

    acc[...] = jnp.zeros_like(acc)

    def cross_chunk(c):
        receive(0, c).wait_recv()
        receive(1, c).wait_recv()
        for i, (x, y) in enumerate(((inbox[0, rows_of(c), :], mine[1, rows_of(c), :]),
                                    (mine[0, rows_of(c), :], inbox[1, rows_of(c), :]))):
            x = jnp.concatenate(split(x), axis=1)
            y = jnp.concatenate(split(y), axis=1)
            acc[i] += dot_t(x, y)

    each(m_chunks, cross_chunk)
    for i in range(2):
        z = acc[i]
        rs2src[:, i * H : (i + 1) * H] = z[0:H, 0:H] + ((z[0:H, H:W] + z[H:W, 0:H]) + z[H:W, H:W])
    total = scatter(rs2src, rs2, rs2_send, rs2_recv)
    ag2[0, mine_rows, :] = total[:, 0:H]
    ag2[1, mine_rows, :] = total[:, H:W]
    for side in range(2):
        send_diag(side).wait_send()
        receive_diag(side).wait_recv()

    copies = []
    for d in range(1, n_rows):
        copies.append(
            pltpu.make_async_remote_copy(
                src_ref=ag2.at[:, mine_rows], dst_ref=ag2.at[:, mine_rows],
                send_sem=ag2_send.at[d], recv_sem=ag2_recv.at[d],
                device_id=(peer(d), k), device_id_type=MESH,
            )
        )
    for copy in copies:
        copy.start()
    for copy in copies:
        copy.wait()

    xl, xr, dl, dr = ag2[0], ag2[1], ag2[2], ag2[3]
    xl_t, xr_t = jnp.transpose(xl), jnp.transpose(xr)
    du, dv = diag[0], diag[1]
    jacobi_start(
        state_a, jnp.where(first, dv, dl), jnp.where(first, xl_t, xl), jnp.where(first, xl, xl_t),
        jnp.where(first, dl, dv),
    )
    jacobi_start(
        state_b, jnp.where(last, dr, du), jnp.where(last, xr_t, xr), jnp.where(last, xr, xr_t),
        jnp.where(last, du, dr),
    )

    def both(t):
        jacobi_step(state_a)
        jacobi_step(state_b)

    each(STEPS, both)

    def weights(state, take_right, flip):
        parts = []
        for q in basis_split(state, sel):
            q = q.astype(F32)
            q = jnp.where(take_right, q[:, H:W], q[:, 0:H])
            up = jnp.where(flip, q[H:W], q[0:H])
            down = jnp.where(flip, q[0:H], q[H:W])
            parts.append(jnp.concatenate([up, down], axis=0).astype(BF16))
        return parts

    wl_hi, wl_lo = weights(state_a, second, first)
    wr_hi, wr_lo = weights(state_b, jnp.logical_not(last), jnp.logical_not(last))

    def finish_chunk(c):
        for i, (w_hi, w_lo) in enumerate(((wl_hi, wl_lo), (wr_hi, wr_lo))):
            x = jnp.concatenate([inbox[i, rows_of(c), :], mine[1 - i, rows_of(c), :]], axis=1)
            hi, lo = split(x)
            panel[rows_of(c), i * H : (i + 1) * H] = dot(hi, w_hi) + (dot(hi, w_lo) + dot(lo, w_hi))

    def out_m(c):
        return pltpu.make_async_copy(panel.at[rows_of(c)], matrix_out.at[rows_of(c)], out_sem.at[c])

    def out_v(c):
        return pltpu.make_async_copy(
            panel.at[rows_of(m_chunks + c)], vectors_out.at[rows_of(c)], out_sem.at[m_chunks + c]
        )

    def finish_m(c):
        finish_chunk(c)
        out_m(c).start()

    def finish_v(c):
        receive(0, m_chunks + c).wait_recv()
        receive(1, m_chunks + c).wait_recv()
        finish_chunk(m_chunks + c)
        out_v(c).start()

    each(m_chunks, finish_m)
    each(v_chunks, finish_v)
    each(chunks, lambda c: send(0, c).wait_send())
    each(chunks, lambda c: send(1, c).wait_send())
    each(m_chunks, lambda c: out_m(c).wait())
    each(v_chunks, lambda c: out_v(c).wait())


def solution(mesh):
    n_rows, n_pairs = mesh.shape["rows"], mesh.shape["pairs"]

    def per_device(matrix, vectors):
        m_rows, v_rows = matrix.shape[0], vectors.shape[0]
        rows = m_rows + v_rows
        chunks = rows // CHUNK
        piece = H // n_rows
        dma = pltpu.SemaphoreType.DMA
        return pl.pallas_call(
            functools.partial(kernel, n_rows, n_pairs, m_rows, v_rows),
            out_shape=(
                jax.ShapeDtypeStruct(matrix.shape, F32),
                jax.ShapeDtypeStruct(vectors.shape, F32),
            ),
            in_specs=[pl.BlockSpec(memory_space=pl.ANY)] * 2,
            out_specs=(pl.BlockSpec(memory_space=pl.ANY),) * 2,
            scratch_shapes=[
                pltpu.VMEM((rows, W), F32),
                pltpu.VMEM((2, rows, H), F32),
                pltpu.VMEM((2, rows, H), F32),
                pltpu.VMEM((2, W, W), F32),
                pltpu.VMEM((H, 3 * H), F32),
                pltpu.VMEM((n_rows, piece, 3 * H), F32),
                pltpu.VMEM((H, 3 * H), F32),
                pltpu.VMEM((2, H, H), F32),
                pltpu.VMEM((H, W), F32),
                pltpu.VMEM((n_rows, piece, W), F32),
                pltpu.VMEM((4, H, H), F32),
            ]
            + [pltpu.VMEM((W, H), F32)] * 8
            + [dma((chunks,)), dma((chunks,)), dma((2, chunks)), dma((2, chunks))]
            + [dma((n_rows,))] * 4
            + [dma((2,))] * 2
            + [dma((n_rows,))] * 4,
            compiler_params=pltpu.CompilerParams(
                collective_id=0, has_side_effects=True, vmem_limit_bytes=48 * 2**20
            ),
        )(matrix, vectors)

    spec = P("rows", "pairs")
    return jax.shard_map(per_device, mesh=mesh, in_specs=(spec, spec), out_specs=(spec, spec), check_vma=False)
```

```python
import functools

import jax
import jax.numpy as jnp
from jax import lax
from jax.experimental import pallas as pl
from jax.experimental.pallas import tpu as pltpu
from jax.sharding import PartitionSpec as P

STEPS = 16
H = 128
W = 2 * H
CHUNK = 256
MESH = pl.DeviceIdType.MESH
F32 = jnp.float32
BF16 = jnp.bfloat16


def iota(shape, axis):
    return lax.broadcasted_iota(jnp.int32, shape, axis)


def split(v):
    hi = v.astype(BF16)
    return hi, (v - hi.astype(F32)).astype(BF16)


def split3(v):
    hi = v.astype(BF16)
    rest = v - hi.astype(F32)
    mid = rest.astype(BF16)
    return hi, mid, (rest - mid.astype(F32)).astype(BF16)


def dot(a, b):
    return jnp.dot(a, b, preferred_element_type=F32)


def dot_t(a, b):
    return lax.dot_general(a, b, (((0,), (0,)), ((), ())), preferred_element_type=F32)


def diag_row(block):
    lane = iota((8, H), 1)
    sub = iota((8, H), 0)
    parts = []
    for g in range(4):
        acc = block[32 * g : 32 * g + 8]
        for i in range(4 * g + 1, 4 * g + 4):
            acc = jnp.where(lane // 8 == i, block[8 * i : 8 * i + 8], acc)
        parts.append(acc)
    low = jnp.where(lane < 32, parts[0], parts[1])
    high = jnp.where(lane < 96, parts[2], parts[3])
    both = jnp.where(lane < 64, low, high)
    return jnp.sum(jnp.where(lane % 8 == sub, both, 0.0), axis=0, keepdims=True)


def angles(x, y):
    m = jnp.maximum(jnp.abs(x), jnp.abs(y))
    g = pl.reciprocal(m, approx=True)
    xs = x * g
    ys = y * g
    s = xs * xs + ys * ys
    r = s * lax.rsqrt(s)
    h = r + jnp.abs(xs)
    w = lax.rsqrt(2.0 * r * h)
    big = h * w
    small = jnp.abs(ys) * w
    flat = x >= 0.0
    none = m == 0.0
    cs = jnp.where(none, 1.0, jnp.where(flat, big, small))
    sn = jnp.where(none, 0.0, jnp.where(flat, small, big))
    return cs, jnp.where(y < 0.0, -sn, sn)


def lane_move(left, right):
    lane0 = iota(left.shape, 1) == 0
    rolled = pltpu.roll(jnp.where(lane0, right, left), 1, 1)
    new_left = jnp.where(lane0, left, rolled)
    new_right = pltpu.roll(jnp.where(lane0, rolled, right), H - 1, 1)
    return new_left, new_right


def as_columns(cs, sn):
    t = jnp.transpose(jnp.where(iota((H, H), 0) < H // 2, cs, sn))
    o = pltpu.roll(t, H // 2, 1)
    near = iota((H, H), 1) < H // 2
    return jnp.where(near, t, o), jnp.where(near, o, t)


def store_rows(ref, up, lo):
    ref[H - 1 : W - 1, :] = lo
    ref[1:H, :] = up[0 : H - 1]
    ref[0:1, :] = up[0:1]
    ref[1:2, :] = lo[0:1]
    ref[W - 1 : W, :] = up[H - 1 : H]


def jacobi_start(state, a, c, c_t, b):
    gl, gr, ql, qr = state
    gl[0:H, :] = a
    gl[H:W, :] = c_t
    gr[0:H, :] = c
    gr[H:W, :] = b
    ql[...] = (iota((W, H), 0) == iota((W, H), 1)).astype(F32)
    qr[...] = (iota((W, H), 0) == iota((W, H), 1) + H).astype(F32)


def jacobi_step(state):
    gl, gr, ql, qr = state
    a, d, c, b = gl[0:H], gl[H:W], gr[0:H], gr[H:W]
    cs, sn = angles(diag_row(a) - diag_row(b), 2.0 * diag_row(c))
    cc, sc = as_columns(cs, sn)
    a, c = lane_move(a * cs + c * sn, c * cs - a * sn)
    d, b = lane_move(d * cs + b * sn, b * cs - d * sn)
    store_rows(gl, a * cc + d * sc, d * cc - a * sc)
    store_rows(gr, c * cc + b * sc, b * cc - c * sc)
    left, right = ql[...], qr[...]
    left, right = lane_move(left * cs + right * sn, right * cs - left * sn)
    ql[...] = left
    qr[...] = right


def home():
    j = iota((W, W), 1)
    at = jnp.where(j < H - STEPS, j + STEPS, 3 * H - STEPS - 1 - j)
    at = jnp.where(j >= H, H + STEPS - j, at)
    at = jnp.where(j >= H + STEPS, j - STEPS, at)
    at = jnp.where(j == 0, 0, at)
    return (iota((W, W), 0) == at).astype(F32).astype(BF16)


def basis_split(state, sel):
    ql, qr = state[2], state[3]
    lh, ll = split(ql[...])
    rh, rl = split(qr[...])
    high = dot(lh, sel[0:H]) + dot(rh, sel[H:W])
    low = dot(ll, sel[0:H]) + dot(rl, sel[H:W])
    return high.astype(BF16), low.astype(BF16)


def gram_blocks(state, sel):
    gl, gr = state[0], state[1]
    moved = sum(dot(l, sel[0:H]) + dot(r, sel[H:W]) for l, r in zip(split3(gl[...]), split3(gr[...])))
    parts = split3(moved)
    top = sum(dot_t(sel[:, 0:H], p[:, 0:H]) for p in parts)
    bottom = sum(dot_t(sel[:, H:W], p[:, H:W]) for p in parts)
    return top, bottom


def kernel(
    n_rows, n_pairs, m_rows, v_rows,
    matrix, vectors, matrix_out, vectors_out,
    panel, other, xy, near, fwd, far, acc, gs, rs1, part1, cross1, ag1, diag, far_diag, rs2src, rs2, part2, cross2, ag2,
    a_gl, a_gr, a_ql, a_qr, b_gl, b_gr, b_ql, b_qr,
    load_sem, out_sem, raw_send, raw_recv, fwd_send, sib_send, far_recv, rs1_send, rs1_recv, ag1_send, ag1_recv,
    rs2_send, rs2_recv, ag2_send, ag2_recv, x1_send, x1_recv, x2_send, x2_recv, dg_send, dg_recv,
):
    me = lax.axis_index("rows")
    k = lax.axis_index("pairs")
    m_chunks, v_chunks = m_rows // CHUNK, v_rows // CHUNK
    chunks = m_chunks + v_chunks
    n_y = n_rows // 2
    y = lax.rem(me, n_y)
    across = lax.rem(me + n_y, n_rows)
    piece = H // n_y
    mine_rows = pl.ds(pl.multiple_of(y * piece, piece), piece)

    side = lax.rem(k // 2, 2)
    low = side == 0
    step = jnp.where(low, 2, -2)
    partner = k + step
    sibling = k + 1 - 2 * lax.rem(k, 2)
    begins, ends = k < 4, k >= n_pairs - 4
    has_fwd = jnp.where(low, jnp.where(ends, 0, 1), jnp.where(begins, 0, 1)) == 1
    has_sib = jnp.where(low, jnp.where(begins, 1, 0), jnp.where(ends, 1, 0)) == 1
    fwd_to = jnp.where(has_fwd, k + 2 * step, sibling)
    x_is_top = jnp.where(low, jnp.where(k == 0, 0, 1), 0) == 1
    px_is_top = jnp.where(low, 0, jnp.where(partner == 0, 0, 1)) == 1
    far_first = jnp.where(low, jnp.where(k == 0, 0, 1), jnp.where(k == n_pairs - 1, 1, 0)) == 1
    far_takes_top = jnp.where(low, jnp.where(k == 1, 0, 1), jnp.where(k == n_pairs - 1, 1, 0)) == 1

    def rows_of(c):
        return pl.ds(pl.multiple_of(c * CHUNK, CHUNK), CHUNK)

    def each(n, body, start=0):
        lax.fori_loop(start, n, lambda i, carry: (body(i), carry)[1], 0)

    def load_m(c):
        return pltpu.make_async_copy(matrix.at[rows_of(c)], panel.at[rows_of(c)], load_sem.at[c])

    def load_v(c):
        at = rows_of(m_chunks + c)
        return pltpu.make_async_copy(vectors.at[rows_of(c)], panel.at[at], load_sem.at[m_chunks + c])

    def raw_m(c):
        return pltpu.make_async_remote_copy(
            src_ref=matrix.at[rows_of(c)], dst_ref=other.at[rows_of(c)], send_sem=raw_send.at[c],
            recv_sem=raw_recv.at[c], device_id=(me, partner), device_id_type=MESH,
        )

    def raw_v(c):
        at = rows_of(m_chunks + c)
        return pltpu.make_async_remote_copy(
            src_ref=vectors.at[rows_of(c)], dst_ref=other.at[at], send_sem=raw_send.at[m_chunks + c],
            recv_sem=raw_recv.at[m_chunks + c], device_id=(me, partner), device_id_type=MESH,
        )

    def raw_in(c):
        return pltpu.make_async_remote_copy(
            src_ref=panel.at[rows_of(c)], dst_ref=other.at[rows_of(c)], send_sem=raw_send.at[c],
            recv_sem=raw_recv.at[c], device_id=(me, partner), device_id_type=MESH,
        )

    def forward(c):
        return pltpu.make_async_remote_copy(
            src_ref=fwd.at[rows_of(c)], dst_ref=far.at[rows_of(c)], send_sem=fwd_send.at[c],
            recv_sem=far_recv.at[c], device_id=(me, fwd_to), device_id_type=MESH,
        )

    def to_sibling(c):
        return pltpu.make_async_remote_copy(
            src_ref=xy.at[1, rows_of(c)], dst_ref=far.at[rows_of(c)], send_sem=sib_send.at[c],
            recv_sem=far_recv.at[c], device_id=(me, sibling), device_id_type=MESH,
        )

    each(m_chunks, lambda c: load_m(c).start())
    each(v_chunks, lambda c: load_v(c).start())

    barrier = pltpu.get_barrier_semaphore()

    def greet(row, pair):
        pl.semaphore_signal(barrier, inc=1, device_id=(row, pair), device_id_type=MESH)

    def y_peer(d):
        return lax.rem(y + d, n_y)

    def peer(d):
        return me - y + y_peer(d)

    for d in range(1, n_y):
        greet(peer(d), k)
    greet(across, k)
    greet(across, partner)
    greet(me, partner)
    greet(me, sibling)

    @pl.when(jnp.logical_not(begins))
    def _():
        greet(me, k - 4)

    @pl.when(jnp.logical_not(ends))
    def _():
        greet(me, k + 4)

    pl.semaphore_wait(barrier, n_y + 3 + jnp.where(begins, 0, 1) + jnp.where(ends, 0, 1))
    raw_m(0).start()
    raw_m(1).start()

    acc[...] = jnp.zeros_like(acc)

    def gram_chunk(c):
        load_m(c).wait()
        hi, lo = split(panel[rows_of(c), :])
        acc[0] += dot_t(hi, hi)
        acc[1] += dot_t(hi, lo)

    each(m_chunks, gram_chunk)
    hl = acc[1]
    full = acc[0] + (hl + jnp.transpose(hl))
    gs[:, 0:H] = full[0:H, 0:H]
    gs[:, H:W] = full[0:H, H:W]
    gs[:, W:] = full[H:W, H:W]

    def scatter(src, dst, send, recv):
        copies = []
        for d in range(1, n_y):
            rows = pl.ds(pl.multiple_of(y_peer(d) * piece, piece), piece)
            copies.append(
                pltpu.make_async_remote_copy(
                    src_ref=src.at[rows], dst_ref=dst.at[d - 1], send_sem=send.at[d], recv_sem=recv.at[d],
                    device_id=(peer(d), k), device_id_type=MESH,
                )
            )
        for copy in copies:
            copy.start()
        for copy in copies:
            copy.wait()
        total = src[mine_rows, :]
        for d in range(1, n_y):
            total = total + dst[d - 1]
        return total

    def gather(part, send, recv):
        copies = []
        for d in range(1, n_y):
            copies.append(
                pltpu.make_async_remote_copy(
                    src_ref=part, dst_ref=part, send_sem=send.at[d], recv_sem=recv.at[d],
                    device_id=(peer(d), k), device_id_type=MESH,
                )
            )
        for copy in copies:
            copy.start()
        for copy in copies:
            copy.wait()

    part1[...] = scatter(gs, rs1, rs1_send, rs1_recv)
    copies = []
    for i, to in enumerate(((across, k), (me, partner), (across, partner))):
        copies.append(
            pltpu.make_async_remote_copy(
                src_ref=part1, dst_ref=cross1.at[i], send_sem=x1_send.at[i], recv_sem=x1_recv.at[i],
                device_id=to, device_id_type=MESH,
            )
        )
    for copy in copies:
        copy.start()
    for copy in copies:
        copy.wait()
    each(m_chunks, lambda c: raw_m(c).start(), start=2)
    raw_v(0).start()
    ag1[0, mine_rows, :] = part1[...] + cross1[0]
    ag1[1, mine_rows, :] = cross1[1] + cross1[2]
    gather(ag1.at[:, mine_rows], ag1_send, ag1_recv)

    state_a = (a_gl, a_gr, a_ql, a_qr)
    state_b = (b_gl, b_gr, b_ql, b_qr)
    for i, state in enumerate((state_a, state_b)):
        c1 = ag1[i, :, H:W]
        jacobi_start(state, ag1[i, :, 0:H], c1, jnp.transpose(c1), ag1[i, :, W:])

    def both(t):
        jacobi_step(state_a)
        jacobi_step(state_b)

    each(STEPS, both)
    sel = home()

    def xy_order(state, top_first):
        parts = []
        for q in basis_split(state, sel):
            q = q.astype(F32)
            left = jnp.where(top_first, q[:, 0:H], q[:, H:W])
            right = jnp.where(top_first, q[:, H:W], q[:, 0:H])
            parts.append(jnp.concatenate([left, right], axis=1).astype(BF16))
        return parts

    def product(x, w_hi, w_lo):
        hi, lo = split(x)
        return dot(hi, w_hi) + (dot(hi, w_lo) + dot(lo, w_hi))

    each(v_chunks, lambda c: load_v(c).wait())
    q_hi, q_lo = xy_order(state_a, x_is_top)

    def rotate_mine(c):
        new = product(panel[rows_of(c), :], q_hi, q_lo)
        xy[0, rows_of(c), :] = new[:, 0:H]
        xy[1, rows_of(c), :] = new[:, H:W]

        @pl.when(has_sib)
        def _():
            to_sibling(c).start()

    each(chunks, rotate_mine)

    for i, (state, top_first) in enumerate(((state_a, x_is_top), (state_b, px_is_top))):
        top, bottom = gram_blocks(state, sel)
        diag[2 * i] = jnp.where(top_first, top, bottom)
        diag[2 * i + 1] = jnp.where(top_first, bottom, top)

    def send_diag(i, to):
        return pltpu.make_async_remote_copy(
            src_ref=diag.at[2 * i + 1], dst_ref=far_diag, send_sem=dg_send.at[i], recv_sem=dg_recv,
            device_id=(me, to), device_id_type=MESH,
        )

    @pl.when(has_sib)
    def _():
        send_diag(0, sibling).start()

    @pl.when(has_fwd)
    def _():
        send_diag(1, fwd_to).start()

    p_hi, p_lo = xy_order(state_b, px_is_top)

    def rotate_other(c):
        raw_in(c).wait_recv()
        new = product(other[rows_of(c), :], p_hi, p_lo)
        fwd[rows_of(c), :] = new[:, H:W]
        near[rows_of(c), :] = new[:, 0:H]

        @pl.when(has_fwd)
        def _():
            forward(c).start()

    acc[...] = jnp.zeros_like(acc)

    def cross(i, half, c):
        x = jnp.concatenate(split(xy[i, rows_of(c), :]), axis=1)
        y = jnp.concatenate(split(half[rows_of(c), :]), axis=1)
        acc[i] += dot_t(x, y)

    def far_cross(c):
        forward(c).wait_recv()
        cross(1, far, c)

    def round_chunk(c):
        rotate_other(c)
        cross(0, near, c)

        @pl.when(c > 0)
        def _():
            far_cross(c - 1)

    each(m_chunks, round_chunk)
    far_cross(m_chunks - 1)
    for i in range(2):
        z = acc[i]
        rs2src[:, i * H : (i + 1) * H] = z[0:H, 0:H] + ((z[0:H, H:W] + z[H:W, 0:H]) + z[H:W, H:W])
    part2[...] = scatter(rs2src, rs2, rs2_send, rs2_recv)
    copy = pltpu.make_async_remote_copy(
        src_ref=part2, dst_ref=cross2, send_sem=x2_send, recv_sem=x2_recv, device_id=(across, k), device_id_type=MESH
    )
    copy.start()
    each(v_chunks, lambda c: raw_v(c).start(), start=1)
    copy.wait()
    ag2[mine_rows, :] = part2[...] + cross2[...]
    gather(ag2.at[mine_rows], ag2_send, ag2_recv)
    send_diag(0, sibling).wait_recv()

    def start_pair(state, mine_first, mine, theirs, z):
        z_t = jnp.transpose(z)
        jacobi_start(
            state, jnp.where(mine_first, mine, theirs), jnp.where(mine_first, z, z_t),
            jnp.where(mine_first, z_t, z), jnp.where(mine_first, theirs, mine),
        )

    start_pair(state_a, low, diag[0], diag[2], ag2[:, 0:H])
    start_pair(state_b, jnp.logical_not(far_first), diag[1], far_diag[...], ag2[:, H:W])
    each(STEPS // 2, both)
    rotate_other(m_chunks)
    each(STEPS // 2, both)
    each(chunks, rotate_other, start=m_chunks + 1)

    def weights(state, take_top, theirs_first):
        parts = []
        for q in basis_split(state, sel):
            q = q.astype(F32)
            q = jnp.where(take_top, q[:, 0:H], q[:, H:W])
            up = jnp.where(theirs_first, q[0:H], q[H:W])
            down = jnp.where(theirs_first, q[H:W], q[0:H])
            parts.append(jnp.concatenate([up, down], axis=0).astype(BF16))
        return parts

    wn_hi, wn_lo = weights(state_a, jnp.logical_not(low), jnp.logical_not(low))
    wf_hi, wf_lo = weights(state_b, far_takes_top, far_first)
    near_cols = pl.ds(pl.multiple_of((1 - side) * H, H), H)
    far_cols = pl.ds(pl.multiple_of(side * H, H), H)

    def finish_chunk(c):
        x = jnp.concatenate([near[rows_of(c), :], xy[0, rows_of(c), :]], axis=1)
        panel[rows_of(c), near_cols] = product(x, wn_hi, wn_lo)
        x = jnp.concatenate([far[rows_of(c), :], xy[1, rows_of(c), :]], axis=1)
        panel[rows_of(c), far_cols] = product(x, wf_hi, wf_lo)

    def out_m(c):
        return pltpu.make_async_copy(panel.at[rows_of(c)], matrix_out.at[rows_of(c)], out_sem.at[c])

    def out_v(c):
        return pltpu.make_async_copy(
            panel.at[rows_of(m_chunks + c)], vectors_out.at[rows_of(c)], out_sem.at[m_chunks + c]
        )

    def finish_m(c):
        finish_chunk(c)
        out_m(c).start()

    def finish_v(c):
        forward(m_chunks + c).wait_recv()
        finish_chunk(m_chunks + c)
        out_v(c).start()

    each(m_chunks, finish_m)
    each(v_chunks, finish_v)

    each(m_chunks, lambda c: raw_m(c).wait_send())
    each(v_chunks, lambda c: raw_v(c).wait_send())

    @pl.when(has_fwd)
    def _():
        each(chunks, lambda c: forward(c).wait_send())
        send_diag(1, fwd_to).wait_send()

    @pl.when(has_sib)
    def _():
        each(chunks, lambda c: to_sibling(c).wait_send())
        send_diag(0, sibling).wait_send()

    each(m_chunks, lambda c: out_m(c).wait())
    each(v_chunks, lambda c: out_v(c).wait())


def solution(mesh):
    n_rows, n_pairs = mesh.shape["rows"], mesh.shape["pairs"]

    def per_device(matrix, vectors):
        m_rows, v_rows = matrix.shape[0], vectors.shape[0]
        rows = m_rows + v_rows
        chunks = rows // CHUNK
        n_y = n_rows // 2
        piece = H // n_y
        dma = pltpu.SemaphoreType.DMA
        vmem = [
            (rows, W), (rows, W), (2, rows, H), (rows, H), (rows, H), (rows, H), (2, W, W),
            (H, 3 * H), (n_y - 1, piece, 3 * H), (piece, 3 * H), (3, piece, 3 * H), (2, H, 3 * H),
            (4, H, H), (H, H), (H, W), (n_y - 1, piece, W), (piece, W), (piece, W), (H, W),
        ] + [(W, H)] * 8
        sems = [chunks] * 7 + [n_y] * 8 + [3, 3, None, None, 2, None]
        return pl.pallas_call(
            functools.partial(kernel, n_rows, n_pairs, m_rows, v_rows),
            out_shape=(
                jax.ShapeDtypeStruct(matrix.shape, F32),
                jax.ShapeDtypeStruct(vectors.shape, F32),
            ),
            in_specs=[pl.BlockSpec(memory_space=pl.ANY)] * 2,
            out_specs=(pl.BlockSpec(memory_space=pl.ANY),) * 2,
            scratch_shapes=[pltpu.VMEM(shape, F32) for shape in vmem]
            + [dma if n is None else dma((n,)) for n in sems],
            compiler_params=pltpu.CompilerParams(
                collective_id=0, has_side_effects=True, vmem_limit_bytes=60 * 2**20
            ),
        )(matrix, vectors)

    spec = P("rows", "pairs")
    return jax.shard_map(per_device, mesh=mesh, in_specs=(spec, spec), out_specs=(spec, spec), check_vma=False)
```
